32 devices in a mesh: replica: 8 (over z, x), expert: 4 (over y, core).
Axes of the slice: x: 2, y: 2, z: 4, core: 2. Of those that a mesh axis runs over, the one named last changes fastest.
Arguments:
- master: float32 [8, 4, 4, 64, 768], P('replica', 'expert'), may hold values from -6 to 6
- first_moment: float32 [8, 4, 4, 64, 768], P('replica', 'expert'), may hold values from -4 to 4
- second_moment: float32 [8, 4, 4, 64, 768], P('replica', 'expert'), may hold values from 0.001 to 1
- gradient: bfloat16 [8, 4, 4, 64, 768], P('replica', 'expert'), may hold values from -6 to 6
- scale_exponent: int32 [8, 4, 4, 64, 6], P('replica', 'expert'), may hold values from 3 to 7
- slot_expert: int32 [8, 4, 4], P('replica', 'expert'), may hold values from 0 to 3, each once within a row
- expert_owner: int32 [4], replicated, may hold values from 0 to 3, each once
- serving_weights: bfloat16 [4, 2048, 768], P('expert'), may hold values from -6 to 6
Outputs:
- master_out: float32 [8, 4, 4, 64, 768], P('replica', 'expert')
- first_out: float32 [8, 4, 4, 64, 768], P('replica', 'expert')
- second_out: float32 [8, 4, 4, 64, 768], P('replica', 'expert')
- serving_out: bfloat16 [4, 2048, 768], P('expert')
The draws below stay inside these ranges and needn't reach their ends.
Inputs may be any that keep to these rules, and one draw needn't show every extreme that they name: `slot_expert`: each row along the last dimension names every expert once. `expert_owner`: names every owner once.
All inputs are finite; a program needn't handle non-finite values.
Results may differ from the reference program's by a relative error of at most 0.0015.
Values may be sent and summed in bfloat16 or wider, within the bound.
A program may use at most 64 MiB of HBM per device.

```python
import math
import jax
import jax.numpy as jnp

D_WIN = 2048
F_WIN = 768
BLOCK = 128
EXPERTS = 4
SUB_ROWS = 64
NBLK = 6
N_REPLICA = 8
N_EXPERT = 4


def place_ends(entries, rng, least, high):
    longest = entries.shape.index(max(entries.shape))
    spots = []
    for shift in (0, 1):
        where = [jax.random.randint(jax.random.fold_in(rng, axis), (), 0, length) for axis, length in enumerate(entries.shape)]
        where[longest] = (where[longest] + shift) % entries.shape[longest]
        spots.append(tuple(where))
    return entries.at[spots[0]].set(least).at[spots[1]].set(high)


def levels(rng, shape, cuts, low, high):
    factor_of, own = 1.0, jax.random.fold_in(rng, 6)
    for position, shards_of in cuts:
        steps = jnp.exp(jax.random.uniform(jax.random.fold_in(own, position), (shards_of,), jnp.float32, low / len(cuts), high / len(cuts)))
        factor_of = factor_of * jnp.repeat(steps, shape[position] // shards_of).reshape([-1 if axis == position else 1 for axis in range(len(shape))])
    return factor_of


def bell_draw(stream_key, shape, scale, reach, shards=(), held_as=jnp.bfloat16):
    loudness = levels(stream_key, shape, shards, -0.22, 0.18) if shards else 1.0
    result = jax.random.normal(stream_key, shape, jnp.float32) * scale * loudness
    return jnp.minimum(jnp.maximum(result, -reach), reach).astype(held_as)


def setup_inputs(seed: int = 0) -> dict:
    key_of = jax.random.split(jax.random.key(seed), 9)
    return {
        "master": bell_draw(key_of[0], (N_REPLICA, N_EXPERT, EXPERTS, SUB_ROWS, F_WIN), 1.0, 6.0, ((0, 8), (1, 4)), jnp.float32),
        "first_moment": bell_draw(key_of[1], (N_REPLICA, N_EXPERT, EXPERTS, SUB_ROWS, F_WIN), 0.3, 4.0, ((0, 8), (1, 4)), jnp.float32),
        "second_moment": jnp.clip(jnp.exp(math.log(1.0) - 6.9077552 * jax.random.uniform(key_of[2], (N_REPLICA, N_EXPERT, EXPERTS, SUB_ROWS, F_WIN), jnp.float32) ** levels(key_of[2], (N_REPLICA, N_EXPERT, EXPERTS, SUB_ROWS, F_WIN), ((0, 8), (1, 4)), -0.2, 0.2)), 0.001, 1.0),
        "gradient": bell_draw(key_of[3], (N_REPLICA, N_EXPERT, EXPERTS, SUB_ROWS, F_WIN), 1.0, 6.0, ((0, 8), (1, 4))),
        "scale_exponent": place_ends(jax.random.randint(key_of[4], (N_REPLICA, N_EXPERT, EXPERTS, SUB_ROWS, NBLK), 3, 8), jax.random.fold_in(key_of[4], 1), 3, 7).astype(jnp.int32),
        "slot_expert": jax.vmap(lambda own: jax.random.permutation(own, EXPERTS))(jax.random.split(key_of[5], N_REPLICA * N_EXPERT)).reshape((N_REPLICA, N_EXPERT, EXPERTS)).astype(jnp.int32),
        "expert_owner": jax.random.permutation(key_of[6], EXPERTS).astype(jnp.int32),
        "serving_weights": bell_draw(key_of[7], (EXPERTS, D_WIN, F_WIN), 1.0, 6.0, ((0, 4),)),
    }


def reference(master, first_moment, second_moment, gradient, scale_exponent, slot_expert, expert_owner, serving_weights):
    grad_full = gradient.astype(jnp.float32)
    first_out = 0.9 * first_moment + 0.1 * grad_full
    second_out = 0.95 * second_moment + 0.05 * grad_full * grad_full
    corr_first = 1.0 - 0.9 ** 10
    corr_second = 1.0 - 0.95 ** 10
    update = first_out / corr_first / (jnp.sqrt(second_out / corr_second) + 1e-08) + 0.1 * master
    delta = -0.1 * update
    master_out = master + delta
    scale = jnp.exp2(-scale_exponent.astype(jnp.float32))
    shaped = delta.reshape(delta.shape[:-1] + (NBLK, BLOCK))
    coded = jnp.clip(shaped / scale[..., None], -8.0, 8.0).astype(jnp.bfloat16)
    inverse = jnp.argsort(slot_expert, axis=-1).astype(jnp.int32)
    coded_by = jnp.take_along_axis(coded, inverse[:, :, :, None, None, None], axis=2)
    scale_by = jnp.take_along_axis(scale, inverse[:, :, :, None, None], axis=2)
    coded_by = jnp.transpose(coded_by, (2, 0, 1, 3, 4, 5)).reshape(EXPERTS, D_WIN, NBLK, BLOCK)
    scale_by = jnp.transpose(scale_by, (2, 0, 1, 3, 4)).reshape(EXPERTS, D_WIN, NBLK)
    served = jnp.argsort(expert_owner).astype(jnp.int32)
    coded_own = coded_by[served]
    scale_own = scale_by[served]
    added = coded_own.astype(jnp.float32) * scale_own[..., None]
    serving_out = (serving_weights.astype(jnp.float32) + added.reshape(EXPERTS, D_WIN, F_WIN)).astype(jnp.bfloat16)
    return (master_out, first_out, second_out, serving_out)
```

```python
import functools

import jax
import jax.numpy as jnp
from jax import lax
from jax.experimental import pallas as pl
from jax.experimental.pallas import tpu as pltpu
from jax.sharding import PartitionSpec as P

MESH = pl.DeviceIdType.MESH
CORES = 2


def adam(master, first_moment, second_moment, gradient):
    grad_full = gradient.astype(jnp.float32)
    first_out = 0.9 * first_moment + 0.1 * grad_full
    second_out = 0.95 * second_moment + 0.05 * grad_full * grad_full
    corr_first = 1.0 - 0.9**10
    corr_second = 1.0 - 0.95**10
    update = first_out / corr_first / (jnp.sqrt(second_out / corr_second) + 1e-08) + 0.1 * master
    delta = -0.1 * update
    return master + delta, first_out, second_out, delta


def adam_kernel(slot_ref, owner_ref, m_ref, f_ref, s_ref, g_ref, e_ref, mo_ref, fo_ref, so_ref, d_ref):
    columns = m_ref.shape[-1]
    blocks = e_ref.shape[-1]
    width = columns // blocks
    limits = jnp.left_shift(1, 7 - e_ref[0]).astype(jnp.float32) * (8.0 / 128.0)
    for b in range(blocks):
        cols = slice(b * width, (b + 1) * width)
        mo, fo, so, delta = adam(m_ref[0, :, cols], f_ref[0, :, cols], s_ref[0, :, cols], g_ref[0, :, cols])
        mo_ref[0, :, cols] = mo
        fo_ref[0, :, cols] = fo
        so_ref[0, :, cols] = so
        limit = limits[:, b : b + 1]
        d_ref[0, :, cols] = jnp.minimum(jnp.maximum(delta, -limit), limit).astype(jnp.bfloat16)


def local_step(slot_expert, expert_owner, master, first_moment, second_moment, gradient, scale_exponent):
    slots, rows, columns = master.shape
    blocks = scale_exponent.shape[-1]
    here = pl.BlockSpec((1, rows, columns), lambda s, se, eo: (s, 0, 0))
    small = pl.BlockSpec((1, rows, blocks), lambda s, se, eo: (s, 0, 0))
    owned = pl.BlockSpec((1, rows, columns), lambda s, se, eo: (eo[se[s]], 0, 0))
    flat = jax.ShapeDtypeStruct(master.shape, jnp.float32)
    return pl.pallas_call(
        adam_kernel,
        grid_spec=pltpu.PrefetchScalarGridSpec(
            num_scalar_prefetch=2,
            grid=(slots,),
            in_specs=[here, here, here, here, small],
            out_specs=[here, here, here, owned],
        ),
        out_shape=[flat, flat, flat, jax.ShapeDtypeStruct(master.shape, jnp.bfloat16)],
        name="adam_step",
    )(slot_expert, expert_owner, master, first_moment, second_moment, gradient, scale_exponent)


def ring_position(index, count):
    return (index // 2) * (1 - index % 2) + (count - 1 - index // 2) * (index % 2)


def ring_index(position, count):
    back = position // (count // 2)
    return 2 * position * (1 - back) + (2 * (count - 1 - position) + 1) * back


def exchange_kernel(n_rep, n_exp, d_ref, out_ref, own_sem, p_send, p_recv, r_send, r_recv):
    rep = lax.axis_index("replica")
    exp = lax.axis_index("expert")
    pos = ring_position(rep, n_rep)
    ahead = ring_index((pos + 1) % n_rep, n_rep)
    behind = ring_index((pos + n_rep - 1) % n_rep, n_rep)
    chips = n_exp // CORES
    chip, core = exp // CORES, exp % CORES

    def peer(k, sign):
        dc, dk = k // CORES, k % CORES
        return ((chip + sign * dc + chips) % chips) * CORES + (core + sign * dk + CORES) % CORES

    barrier = pltpu.get_barrier_semaphore()
    for k in range(1, n_exp):
        pl.semaphore_signal(barrier, inc=1, device_id=(rep, peer(k, 1)), device_id_type=MESH)
    for near in (ahead, behind):
        pl.semaphore_signal(barrier, inc=1, device_id=(near, exp), device_id_type=MESH)
    own = pltpu.make_async_copy(d_ref.at[exp], out_ref.at[rep, exp], own_sem)
    own.start()
    pl.semaphore_wait(barrier, n_exp + 1)

    swaps = {}
    for k in list(range(CORES, n_exp)) + list(range(1, CORES)):
        swaps[k] = pltpu.make_async_remote_copy(
            src_ref=d_ref.at[peer(k, 1)],
            dst_ref=out_ref.at[rep, exp],
            send_sem=p_send.at[k],
            recv_sem=p_recv.at[k],
            device_id=(rep, peer(k, 1)),
            device_id_type=MESH,
        )
        swaps[k].start()

    far, near = n_rep // 2, n_rep - 1 - n_rep // 2
    hops = [[far if (k % 4 in (0, 3)) == (way == 0) else near for k in range(n_exp)] for way in (0, 1)]

    def ring(way, h, k):
        step = h if way == 0 else n_rep - h
        origin = ring_index((pos + n_rep - step) % n_rep, n_rep)
        block = out_ref.at[origin, peer(k, -1)]
        return pltpu.make_async_remote_copy(
            src_ref=block,
            dst_ref=block,
            send_sem=r_send.at[way, h, k],
            recv_sem=r_recv.at[way, h, k],
            device_id=(ahead if way == 0 else behind, exp),
            device_id_type=MESH,
        )

    sent = []
    for h in range(far):
        for k in range(n_exp):
            if h == 0:
                if k == 0:
                    own.wait()
                else:
                    swaps[k].wait_recv()
            for way in (0, 1):
                if h and h - 1 < hops[way][k]:
                    ring(way, h - 1, k).wait_recv()
                if h < hops[way][k]:
                    copy = ring(way, h, k)
                    copy.start()
                    sent.append(copy)
    for way in (0, 1):
        for k in range(n_exp):
            if hops[way][k] == far:
                ring(way, far - 1, k).wait_recv()
    for k in range(1, n_exp):
        swaps[k].wait_send()
    for copy in sent:
        copy.wait_send()


def exchange(n_rep, n_exp, delta):
    slots, rows, columns = delta.shape
    size = n_rep * n_exp * rows * columns * 2
    far = n_rep // 2
    return pl.pallas_call(
        functools.partial(exchange_kernel, n_rep, n_exp),
        out_shape=jax.ShapeDtypeStruct((n_rep, n_exp, rows, columns), jnp.bfloat16),
        in_specs=[pl.BlockSpec(memory_space=pltpu.VMEM)],
        out_specs=pl.BlockSpec(memory_space=pltpu.VMEM),
        scratch_shapes=[
            pltpu.SemaphoreType.DMA(()),
            pltpu.SemaphoreType.DMA((n_exp,)),
            pltpu.SemaphoreType.DMA((n_exp,)),
            pltpu.SemaphoreType.DMA((2, far, n_exp)),
            pltpu.SemaphoreType.DMA((2, far, n_exp)),
        ],
        compiler_params=pltpu.CompilerParams(
            collective_id=0, has_side_effects=True, vmem_limit_bytes=24 * 1024 * 1024
        ),
        cost_estimate=pl.CostEstimate(flops=0, bytes_accessed=size, transcendentals=0),
        name="exchange",
    )(delta)


def exchange_by_collectives(delta):
    received = lax.all_to_all(delta, "expert", split_axis=0, concat_axis=0, tiled=True)
    return lax.all_gather(received, "replica", axis=0, tiled=False)


def shards(
    n_rep,
    n_exp,
    master,
    first_moment,
    second_moment,
    gradient,
    scale_exponent,
    slot_expert,
    expert_owner,
    serving_weights,
):
    master_out, first_out, second_out, delta = local_step(
        slot_expert[0, 0],
        expert_owner,
        master[0, 0],
        first_moment[0, 0],
        second_moment[0, 0],
        gradient[0, 0],
        scale_exponent[0, 0],
    )
    rows = master.shape[3]
    if rows % 16 == 0 and n_rep % 2 == 0 and n_exp % CORES == 0:
        gathered = exchange(n_rep, n_exp, delta)
    else:
        gathered = exchange_by_collectives(delta)
    added = gathered.reshape(serving_weights.shape).astype(jnp.float32)
    serving_out = (serving_weights.astype(jnp.float32) + added).astype(jnp.bfloat16)
    return (master_out[None, None], first_out[None, None], second_out[None, None], serving_out)


def solution(mesh):
    flat = P("replica", "expert", None, None, None)
    in_specs = (flat, flat, flat, flat, flat, P("replica", "expert", None), P(), P("expert", None, None))
    out_specs = (flat, flat, flat, P("expert", None, None))
    body = functools.partial(shards, mesh.shape["replica"], mesh.shape["expert"])
    return jax.shard_map(body, mesh=mesh, in_specs=in_specs, out_specs=out_specs, check_vma=False)
```

```python
import functools

import jax
import jax.numpy as jnp
from jax import lax
from jax.experimental import pallas as pl
from jax.experimental.pallas import tpu as pltpu
from jax.sharding import PartitionSpec as P

MESH = pl.DeviceIdType.MESH
CORES = 2


def adam(master, first_moment, second_moment, gradient):
    grad_full = gradient.astype(jnp.float32)
    first_out = 0.9 * first_moment + 0.1 * grad_full
    second_out = 0.95 * second_moment + 0.05 * grad_full * grad_full
    corr_first = 1.0 / (1.0 - 0.9**10)
    corr_second = 1.0 / (1.0 - 0.95**10)
    update = first_out * corr_first / (jnp.sqrt(second_out * corr_second) + 1e-08) + 0.1 * master
    delta = -0.1 * update
    return master + delta, first_out, second_out, delta


def adam_kernel(slot_ref, owner_ref, m_ref, f_ref, s_ref, g_ref, e_ref, mo_ref, fo_ref, so_ref, d_ref):
    columns = m_ref.shape[-1]
    blocks = e_ref.shape[0]
    width = columns // blocks
    exponent = e_ref[:, pl.ds(pl.program_id(0), 1), :][:, 0, :]
    limits = (jnp.left_shift(1, 7 - exponent).astype(jnp.float32) * (8.0 / 128.0)).T
    for b in range(blocks):
        cols = slice(b * width, (b + 1) * width)
        mo, fo, so, delta = adam(m_ref[0, :, cols], f_ref[0, :, cols], s_ref[0, :, cols], g_ref[0, :, cols])
        mo_ref[0, :, cols] = mo
        fo_ref[0, :, cols] = fo
        so_ref[0, :, cols] = so
        limit = limits[:, b : b + 1]
        d_ref[0, :, cols] = jnp.minimum(jnp.maximum(delta, -limit), limit).astype(jnp.bfloat16)


def local_step(slot_expert, expert_owner, master, first_moment, second_moment, gradient, scale_exponent):
    slots, rows, columns = master.shape
    by_block = jnp.transpose(scale_exponent, (2, 0, 1))
    here = pl.BlockSpec((1, rows, columns), lambda s, se, eo: (s, 0, 0))
    whole = pl.BlockSpec(by_block.shape, lambda s, se, eo: (0, 0, 0))
    owned = pl.BlockSpec((1, rows, columns), lambda s, se, eo: (eo[se[s]], 0, 0))
    flat = jax.ShapeDtypeStruct(master.shape, jnp.float32)
    return pl.pallas_call(
        adam_kernel,
        grid_spec=pltpu.PrefetchScalarGridSpec(
            num_scalar_prefetch=2,
            grid=(slots,),
            in_specs=[here, here, here, here, whole],
            out_specs=[here, here, here, owned],
        ),
        out_shape=[flat, flat, flat, jax.ShapeDtypeStruct(master.shape, jnp.bfloat16)],
        name="adam_step",
    )(slot_expert, expert_owner, master, first_moment, second_moment, gradient, by_block)


def ring_position(index, count):
    return (index // 2) * (1 - index % 2) + (count - 1 - index // 2) * (index % 2)


def ring_index(position, count):
    back = position // (count // 2)
    return 2 * position * (1 - back) + (2 * (count - 1 - position) + 1) * back


def exchange_kernel(
    n_rep, n_exp, d_ref, w_ref, out_ref, buf, weights, own_sem, w_sem, p_send, p_recv, r_send, r_recv
):
    rep = lax.axis_index("replica")
    exp = lax.axis_index("expert")
    pos = ring_position(rep, n_rep)
    ahead = ring_index((pos + 1) % n_rep, n_rep)
    behind = ring_index((pos + n_rep - 1) % n_rep, n_rep)
    chips = n_exp // CORES
    chip, core = exp // CORES, exp % CORES

    def peer(k, sign):
        dc, dk = k // CORES, k % CORES
        return ((chip + sign * dc + chips) % chips) * CORES + (core + sign * dk + CORES) % CORES

    barrier = pltpu.get_barrier_semaphore()
    for k in range(1, n_exp):
        pl.semaphore_signal(barrier, inc=1, device_id=(rep, peer(k, 1)), device_id_type=MESH)
    for near in (ahead, behind):
        pl.semaphore_signal(barrier, inc=1, device_id=(near, exp), device_id_type=MESH)
    own = pltpu.make_async_copy(d_ref.at[exp], buf.at[rep, exp], own_sem)
    own.start()
    load = pltpu.make_async_copy(w_ref, weights, w_sem)
    load.start()
    pl.semaphore_wait(barrier, n_exp + 1)

    far, near = n_rep // 2, n_rep - 1 - n_rep // 2
    hops = [[far if (k % 4 in (0, 3)) == (way == 0) else near for k in range(n_exp)] for way in (0, 1)]

    def origin(way, h):
        return ring_index((pos + n_rep - (h if way == 0 else n_rep - h)) % n_rep, n_rep)

    def ring(way, h, k):
        block = buf.at[origin(way, h), peer(k, -1)]
        return pltpu.make_async_remote_copy(
            src_ref=d_ref.at[exp] if h == 0 and k == 0 else block,
            dst_ref=block,
            send_sem=r_send.at[way, h, k],
            recv_sem=r_recv.at[way, h, k],
            device_id=(ahead if way == 0 else behind, exp),
            device_id_type=MESH,
        )

    def apply(source, k):
        at = (source, peer(k, -1))
        out_ref[at] = (weights[at].astype(jnp.float32) + buf[at].astype(jnp.float32)).astype(jnp.bfloat16)

    sent = []

    def forward(way, h, k):
        if h < hops[way][k]:
            copy = ring(way, h, k)
            copy.start()
            sent.append(copy)

    for way in (0, 1):
        forward(way, 0, 0)
    swaps = {}
    for k in list(range(CORES, n_exp)) + list(range(1, CORES)):
        swaps[k] = pltpu.make_async_remote_copy(
            src_ref=d_ref.at[peer(k, 1)],
            dst_ref=buf.at[rep, exp],
            send_sem=p_send.at[k],
            recv_sem=p_recv.at[k],
            device_id=(rep, peer(k, 1)),
            device_id_type=MESH,
        )
        swaps[k].start()

    for k in range(1, n_exp):
        swaps[k].wait_recv()
        for way in (0, 1):
            forward(way, 0, k)
    own.wait()
    load.wait()
    for k in range(n_exp):
        apply(rep, k)
    for h in range(1, far + 1):
        for k in range(n_exp):
            for way in (0, 1):
                if h <= hops[way][k]:
                    ring(way, h - 1, k).wait_recv()
                    forward(way, h, k)
                    apply(origin(way, h), k)
    for k in range(1, n_exp):
        swaps[k].wait_send()
    for copy in sent:
        copy.wait_send()


def exchange(n_rep, n_exp, delta, weights):
    slots, rows, columns = delta.shape
    whole = (n_rep, n_exp, rows, columns)
    size = n_rep * n_exp * rows * columns * 2
    far = n_rep // 2
    return pl.pallas_call(
        functools.partial(exchange_kernel, n_rep, n_exp),
        out_shape=jax.ShapeDtypeStruct(whole, jnp.bfloat16),
        in_specs=[pl.BlockSpec(memory_space=pltpu.HBM)] * 2,
        out_specs=pl.BlockSpec(memory_space=pltpu.VMEM),
        scratch_shapes=[
            pltpu.VMEM(whole, jnp.bfloat16),
            pltpu.VMEM(whole, jnp.bfloat16),
            pltpu.SemaphoreType.DMA(()),
            pltpu.SemaphoreType.DMA(()),
            pltpu.SemaphoreType.DMA((n_exp,)),
            pltpu.SemaphoreType.DMA((n_exp,)),
            pltpu.SemaphoreType.DMA((2, far, n_exp)),
            pltpu.SemaphoreType.DMA((2, far, n_exp)),
        ],
        compiler_params=pltpu.CompilerParams(
            collective_id=0, has_side_effects=True, vmem_limit_bytes=50 * 1024 * 1024
        ),
        cost_estimate=pl.CostEstimate(flops=0, bytes_accessed=3 * size, transcendentals=0),
        name="exchange",
    )(delta, weights.reshape(whole))


def exchange_by_collectives(delta):
    received = lax.all_to_all(delta, "expert", split_axis=0, concat_axis=0, tiled=True)
    return lax.all_gather(received, "replica", axis=0, tiled=False)


def shards(
    n_rep,
    n_exp,
    master,
    first_moment,
    second_moment,
    gradient,
    scale_exponent,
    slot_expert,
    expert_owner,
    serving_weights,
):
    master_out, first_out, second_out, delta = local_step(
        slot_expert[0, 0],
        expert_owner,
        master[0, 0],
        first_moment[0, 0],
        second_moment[0, 0],
        gradient[0, 0],
        scale_exponent[0, 0],
    )
    rows = master.shape[3]
    if rows % 16 == 0 and n_rep % 2 == 0 and n_exp % CORES == 0:
        serving_out = exchange(n_rep, n_exp, delta, serving_weights).reshape(serving_weights.shape)
    else:
        added = exchange_by_collectives(delta).reshape(serving_weights.shape).astype(jnp.float32)
        serving_out = (serving_weights.astype(jnp.float32) + added).astype(jnp.bfloat16)
    return (master_out[None, None], first_out[None, None], second_out[None, None], serving_out)


def solution(mesh):
    flat = P("replica", "expert", None, None, None)
    in_specs = (flat, flat, flat, flat, flat, P("replica", "expert", None), P(), P("expert", None, None))
    out_specs = (flat, flat, flat, P("expert", None, None))
    body = functools.partial(shards, mesh.shape["replica"], mesh.shape["expert"])
    return jax.shard_map(body, mesh=mesh, in_specs=in_specs, out_specs=out_specs, check_vma=False)
```

```python
import functools

import jax
import jax.numpy as jnp
from jax import lax
from jax.experimental import pallas as pl
from jax.experimental.pallas import tpu as pltpu
from jax.sharding import PartitionSpec as P

MESH = pl.DeviceIdType.MESH
CORES = 2


def adam(master, first_moment, second_moment, gradient):
    grad_full = gradient.astype(jnp.float32)
    first_out = 0.9 * first_moment + 0.1 * grad_full
    second_out = 0.95 * second_moment + 0.05 * grad_full * grad_full
    corr_first = 1.0 / (1.0 - 0.9**10)
    corr_second = 1.0 / (1.0 - 0.95**10)
    update = first_out * corr_first / (jnp.sqrt(second_out * corr_second) + 1e-08) + 0.1 * master
    delta = -0.1 * update
    return master + delta, first_out, second_out, delta


def adam_kernel(slot_ref, owner_ref, m_ref, f_ref, s_ref, g_ref, e_ref, mo_ref, fo_ref, so_ref, d_ref):
    columns = m_ref.shape[-1]
    blocks = e_ref.shape[0]
    width = columns // blocks
    exponent = e_ref[:, pl.ds(pl.program_id(0), 1), :][:, 0, :]
    limits = (jnp.left_shift(1, 7 - exponent).astype(jnp.float32) * (8.0 / 128.0)).T
    for b in range(blocks):
        cols = slice(b * width, (b + 1) * width)
        mo, fo, so, delta = adam(m_ref[0, :, cols], f_ref[0, :, cols], s_ref[0, :, cols], g_ref[0, :, cols])
        mo_ref[0, :, cols] = mo
        fo_ref[0, :, cols] = fo
        so_ref[0, :, cols] = so
        limit = limits[:, b : b + 1]
        d_ref[0, :, cols] = jnp.minimum(jnp.maximum(delta, -limit), limit).astype(jnp.bfloat16)


def local_step(slot_expert, expert_owner, master, first_moment, second_moment, gradient, scale_exponent):
    slots, rows, columns = master.shape
    by_block = jnp.transpose(scale_exponent, (2, 0, 1))
    here = pl.BlockSpec((1, rows, columns), lambda s, se, eo: (s, 0, 0))
    whole = pl.BlockSpec(by_block.shape, lambda s, se, eo: (0, 0, 0))
    owned = pl.BlockSpec((1, rows, columns), lambda s, se, eo: (eo[se[s]], 0, 0))
    flat = jax.ShapeDtypeStruct(master.shape, jnp.float32)
    return pl.pallas_call(
        adam_kernel,
        grid_spec=pltpu.PrefetchScalarGridSpec(
            num_scalar_prefetch=2,
            grid=(slots,),
            in_specs=[here, here, here, here, whole],
            out_specs=[here, here, here, owned],
        ),
        out_shape=[flat, flat, flat, jax.ShapeDtypeStruct(master.shape, jnp.bfloat16)],
        name="adam_step",
    )(slot_expert, expert_owner, master, first_moment, second_moment, gradient, by_block)


def ring_position(index, count):
    return (index // 2) * (1 - index % 2) + (count - 1 - index // 2) * (index % 2)


def ring_index(position, count):
    back = position // (count // 2)
    return 2 * position * (1 - back) + (2 * (count - 1 - position) + 1) * back


def fused_kernel(
    n_rep, n_exp,
    slot_ref, owner_ref, m_ref, f_ref, s_ref, g_ref, e_ref, w_ref,
    mo_ref, fo_ref, so_ref, out_ref,
    m_in, f_in, s_in, g_in, e_in, m_new, f_new, s_new, d_buf, buf, weights, rows_new,
    in_sem, w_sem, out_sem, rows_sem, p_send, p_recv, r_send, r_recv,
):
    rep = lax.axis_index("replica")
    exp = lax.axis_index("expert")
    pos = ring_position(rep, n_rep)
    ahead = ring_index((pos + 1) % n_rep, n_rep)
    behind = ring_index((pos + n_rep - 1) % n_rep, n_rep)
    chips = n_exp // CORES
    chip, core = exp // CORES, exp % CORES
    columns = m_in.shape[-1]
    blocks = e_in.shape[0]
    width = columns // blocks

    def peer(k, sign):
        dc, dk = k // CORES, k % CORES
        return ((chip + sign * dc + chips) % chips) * CORES + (core + sign * dk + CORES) % CORES

    pairs = ((m_ref, m_in), (f_ref, f_in), (s_ref, s_in), (g_ref, g_in), (e_ref, e_in))
    loads = [pltpu.make_async_copy(src, dst, in_sem.at[i]) for i, (src, dst) in enumerate(pairs)]
    for copy in loads:
        copy.start()
    barrier = pltpu.get_barrier_semaphore()
    for k in range(1, n_exp):
        pl.semaphore_signal(barrier, inc=1, device_id=(rep, peer(k, 1)), device_id_type=MESH)
    for near in (ahead, behind):
        pl.semaphore_signal(barrier, inc=1, device_id=(near, exp), device_id_type=MESH)
    for copy in loads:
        copy.wait()
    load = pltpu.make_async_copy(w_ref, weights, w_sem)
    load.start()

    def prepare(k):
        target = peer(k, 1)
        slot = 0
        for i in range(n_exp):
            slot = jnp.where(owner_ref[slot_ref[i]] == target, i, slot)
        exponent = e_in[:, pl.ds(slot, 1), :][:, 0, :]
        limits = (jnp.left_shift(1, 7 - exponent).astype(jnp.float32) * (8.0 / 128.0)).T
        for b in range(blocks):
            cols = slice(b * width, (b + 1) * width)
            delta = adam(m_in[slot, :, cols], f_in[slot, :, cols], s_in[slot, :, cols], g_in[slot, :, cols])[3]
            limit = limits[:, b : b + 1]
            d_buf[k, :, cols] = jnp.minimum(jnp.maximum(delta, -limit), limit).astype(jnp.bfloat16)

    def state(slot):
        for b in range(blocks):
            at = (slot, slice(None), slice(b * width, (b + 1) * width))
            m_new[at], f_new[at], s_new[at], _ = adam(m_in[at], f_in[at], s_in[at], g_in[at])
        for i, (src, dst) in enumerate(((m_new, mo_ref), (f_new, fo_ref), (s_new, so_ref))):
            stored.append(pltpu.make_async_copy(src.at[slot], dst.at[slot], out_sem.at[i, slot]))
            stored[-1].start()

    stored = []

    far, near = n_rep // 2, n_rep - 1 - n_rep // 2
    hops = [[far if (k % 4 in (0, 3)) == (way == 0) else near for k in range(n_exp)] for way in (0, 1)]

    def origin(way, h):
        return ring_index((pos + n_rep - (h if way == 0 else n_rep - h)) % n_rep, n_rep)

    def ring(way, h, k):
        block = buf.at[origin(way, h), peer(k, -1)]
        return pltpu.make_async_remote_copy(
            src_ref=d_buf.at[0] if h == 0 and k == 0 else block,
            dst_ref=block,
            send_sem=r_send.at[way, h, k],
            recv_sem=r_recv.at[way, h, k],
            device_id=(ahead if way == 0 else behind, exp),
            device_id_type=MESH,
        )

    def apply(source, k, step, own=False):
        at = (source, peer(k, -1))
        added = (d_buf[0] if own else buf[at]).astype(jnp.float32)
        rows_new[at] = (weights[at].astype(jnp.float32) + added).astype(jnp.bfloat16)
        stored.append(pltpu.make_async_copy(rows_new.at[at], out_ref.at[at], rows_sem.at[step, k]))
        stored[-1].start()

    sent = []

    def forward(way, h, k):
        if h < hops[way][k]:
            copy = ring(way, h, k)
            copy.start()
            sent.append(copy)

    prepare(0)
    pl.semaphore_wait(barrier, n_exp + 1)
    for way in (0, 1):
        forward(way, 0, 0)
    swaps = {}
    for k in list(range(1, CORES)) + list(range(CORES, n_exp)):
        prepare(k)
        swaps[k] = pltpu.make_async_remote_copy(
            src_ref=d_buf.at[k],
            dst_ref=buf.at[rep, exp],
            send_sem=p_send.at[k],
            recv_sem=p_recv.at[k],
            device_id=(rep, peer(k, 1)),
            device_id_type=MESH,
        )
        swaps[k].start()

    for k in range(1, n_exp):
        swaps[k].wait_recv()
        for way in (0, 1):
            forward(way, 0, k)
        state(k)
    load.wait()
    state(0)
    for k in range(n_exp):
        apply(rep, k, 0, own=k == 0)
    for h in range(1, far + 1):
        for k in range(n_exp):
            for way in (0, 1):
                if h <= hops[way][k]:
                    ring(way, h - 1, k).wait_recv()
                    forward(way, h, k)
                    apply(origin(way, h), k, 2 * h - 1 + way)
    for k in range(1, n_exp):
        swaps[k].wait_send()
    for copy in sent:
        copy.wait_send()
    for copy in stored:
        copy.wait()


def fused(n_rep, n_exp, slot_expert, expert_owner, master, first, second, gradient, scale_exponent, weights):
    slots, rows, columns = master.shape
    by_block = jnp.transpose(scale_exponent, (2, 0, 1))
    whole = (n_rep, n_exp, rows, columns)
    size = n_rep * n_exp * rows * columns * 2
    far = n_rep // 2
    flat = jax.ShapeDtypeStruct(master.shape, jnp.float32)
    return pl.pallas_call(
        functools.partial(fused_kernel, n_rep, n_exp),
        out_shape=[flat, flat, flat, jax.ShapeDtypeStruct(whole, jnp.bfloat16)],
        in_specs=[pl.BlockSpec(memory_space=pltpu.SMEM)] * 2 + [pl.BlockSpec(memory_space=pl.ANY)] * 6,
        out_specs=[pl.BlockSpec(memory_space=pl.ANY)] * 4,
        scratch_shapes=[
            pltpu.VMEM(master.shape, jnp.float32),
            pltpu.VMEM(master.shape, jnp.float32),
            pltpu.VMEM(master.shape, jnp.float32),
            pltpu.VMEM(master.shape, jnp.bfloat16),
            pltpu.VMEM(by_block.shape, jnp.int32),
            pltpu.VMEM(master.shape, jnp.float32),
            pltpu.VMEM(master.shape, jnp.float32),
            pltpu.VMEM(master.shape, jnp.float32),
            pltpu.VMEM(master.shape, jnp.bfloat16),
            pltpu.VMEM(whole, jnp.bfloat16),
            pltpu.VMEM(whole, jnp.bfloat16),
            pltpu.VMEM(whole, jnp.bfloat16),
            pltpu.SemaphoreType.DMA((5,)),
            pltpu.SemaphoreType.DMA(()),
            pltpu.SemaphoreType.DMA((3, slots)),
            pltpu.SemaphoreType.DMA((2 * far + 1, n_exp)),
            pltpu.SemaphoreType.DMA((n_exp,)),
            pltpu.SemaphoreType.DMA((n_exp,)),
            pltpu.SemaphoreType.DMA((2, far, n_exp)),
            pltpu.SemaphoreType.DMA((2, far, n_exp)),
        ],
        compiler_params=pltpu.CompilerParams(
            collective_id=0, has_side_effects=True, vmem_limit_bytes=60 * 1024 * 1024
        ),
        cost_estimate=pl.CostEstimate(flops=0, bytes_accessed=3 * size, transcendentals=0),
        name="fused_step",
    )(slot_expert, expert_owner, master, first, second, gradient, by_block, weights.reshape(whole))


def exchange_by_collectives(delta):
    received = lax.all_to_all(delta, "expert", split_axis=0, concat_axis=0, tiled=True)
    return lax.all_gather(received, "replica", axis=0, tiled=False)


def shards(
    n_rep,
    n_exp,
    master,
    first_moment,
    second_moment,
    gradient,
    scale_exponent,
    slot_expert,
    expert_owner,
    serving_weights,
):
    state = (
        slot_expert[0, 0],
        expert_owner,
        master[0, 0],
        first_moment[0, 0],
        second_moment[0, 0],
        gradient[0, 0],
        scale_exponent[0, 0],
    )
    rows = master.shape[3]
    if rows % 16 == 0 and n_rep % 2 == 0 and n_exp % CORES == 0:
        master_out, first_out, second_out, new_rows = fused(n_rep, n_exp, *state, serving_weights)
        serving_out = new_rows.reshape(serving_weights.shape)
    else:
        master_out, first_out, second_out, delta = local_step(*state)
        added = exchange_by_collectives(delta).reshape(serving_weights.shape).astype(jnp.float32)
        serving_out = (serving_weights.astype(jnp.float32) + added).astype(jnp.bfloat16)
    return (master_out[None, None], first_out[None, None], second_out[None, None], serving_out)


def solution(mesh):
    flat = P("replica", "expert", None, None, None)
    in_specs = (flat, flat, flat, flat, flat, P("replica", "expert", None), P(), P("expert", None, None))
    out_specs = (flat, flat, flat, P("expert", None, None))
    body = functools.partial(shards, mesh.shape["replica"], mesh.shape["expert"])
    return jax.shard_map(body, mesh=mesh, in_specs=in_specs, out_specs=out_specs, check_vma=False)
```

```python
import functools

import jax
import jax.numpy as jnp
from jax import lax
from jax.experimental import pallas as pl
from jax.experimental.pallas import tpu as pltpu
from jax.sharding import PartitionSpec as P

MESH = pl.DeviceIdType.MESH
CORES = 2


def adam(master, first_moment, second_moment, gradient):
    grad_full = gradient.astype(jnp.float32)
    first_out = 0.9 * first_moment + 0.1 * grad_full
    second_out = 0.95 * second_moment + 0.05 * grad_full * grad_full
    corr_first = 1.0 / (1.0 - 0.9**10)
    corr_second = 1.0 / (1.0 - 0.95**10)
    update = first_out * corr_first / (jnp.sqrt(second_out * corr_second) + 1e-08) + 0.1 * master
    delta = -0.1 * update
    return master + delta, first_out, second_out, delta


def adam_kernel(
    slot_ref, owner_ref, m_ref, f_ref, s_ref, g_ref, e_ref, mo_ref, fo_ref, so_ref, d_ref,
    m_in, f_in, s_in, g_in, e_in, m_new, f_new, s_new, e_sem, in_sem, out_sem,
):
    slots, _, columns = m_in.shape
    blocks = e_in.shape[0]
    width = columns // blocks
    exponents = pltpu.make_async_copy(e_ref, e_in, e_sem)
    exponents.start()
    pairs = ((m_ref, m_in), (f_ref, f_in), (s_ref, s_in), (g_ref, g_in))
    loads = [
        [pltpu.make_async_copy(src.at[s], dst.at[s], in_sem.at[i, s]) for i, (src, dst) in enumerate(pairs)]
        for s in range(slots)
    ]
    for copies in loads:
        for copy in copies:
            copy.start()
    exponents.wait()
    stores = []
    for s, copies in enumerate(loads):
        target = owner_ref[slot_ref[s]]
        limits = (jnp.left_shift(1, 7 - e_in[:, s, :]).astype(jnp.float32) * (8.0 / 128.0)).T
        for copy in copies:
            copy.wait()
        for b in range(blocks):
            cols = slice(b * width, (b + 1) * width)
            at = (s, slice(None), cols)
            m_new[at], f_new[at], s_new[at], delta = adam(m_in[at], f_in[at], s_in[at], g_in[at])
            limit = limits[:, b : b + 1]
            d_ref[target, :, cols] = jnp.minimum(jnp.maximum(delta, -limit), limit).astype(jnp.bfloat16)
        for i, (src, dst) in enumerate(((m_new, mo_ref), (f_new, fo_ref), (s_new, so_ref))):
            stores.append(pltpu.make_async_copy(src.at[s], dst.at[s], out_sem.at[i, s]))
            stores[-1].start()
    for copy in stores:
        copy.wait()


def local_step(slot_expert, expert_owner, master, first_moment, second_moment, gradient, scale_exponent):
    slots = master.shape[0]
    by_block = jnp.transpose(scale_exponent, (2, 0, 1))
    flat = jax.ShapeDtypeStruct(master.shape, jnp.float32)
    held = pltpu.VMEM(master.shape, jnp.float32)
    return pl.pallas_call(
        adam_kernel,
        in_specs=[pl.BlockSpec(memory_space=pltpu.SMEM)] * 2 + [pl.BlockSpec(memory_space=pl.ANY)] * 5,
        out_specs=[pl.BlockSpec(memory_space=pl.ANY)] * 3 + [pl.BlockSpec(memory_space=pltpu.VMEM)],
        out_shape=[flat, flat, flat, jax.ShapeDtypeStruct(master.shape, jnp.bfloat16)],
        scratch_shapes=[
            held,
            held,
            held,
            pltpu.VMEM(master.shape, jnp.bfloat16),
            pltpu.VMEM(by_block.shape, jnp.int32),
            held,
            held,
            held,
            pltpu.SemaphoreType.DMA(()),
            pltpu.SemaphoreType.DMA((4, slots)),
            pltpu.SemaphoreType.DMA((3, slots)),
        ],
        compiler_params=pltpu.CompilerParams(vmem_limit_bytes=107 * 512 * 1024),
        name="adam_step",
    )(slot_expert, expert_owner, master, first_moment, second_moment, gradient, by_block)


def ring_position(index, count):
    return (index // 2) * (1 - index % 2) + (count - 1 - index // 2) * (index % 2)


def ring_index(position, count):
    back = position // (count // 2)
    return 2 * position * (1 - back) + (2 * (count - 1 - position) + 1) * back


def exchange_kernel(
    n_rep, n_exp, d_ref, w_ref, out_ref, buf, weights, own_sem, w_sem, p_send, p_recv, r_send, r_recv
):
    rep = lax.axis_index("replica")
    exp = lax.axis_index("expert")
    pos = ring_position(rep, n_rep)
    ahead = ring_index((pos + 1) % n_rep, n_rep)
    behind = ring_index((pos + n_rep - 1) % n_rep, n_rep)
    chips = n_exp // CORES
    chip, core = exp // CORES, exp % CORES

    def peer(k, sign):
        dc, dk = k // CORES, k % CORES
        return ((chip + sign * dc + chips) % chips) * CORES + (core + sign * dk + CORES) % CORES

    barrier = pltpu.get_barrier_semaphore()
    for k in range(1, n_exp):
        pl.semaphore_signal(barrier, inc=1, device_id=(rep, peer(k, 1)), device_id_type=MESH)
    for near in (ahead, behind):
        pl.semaphore_signal(barrier, inc=1, device_id=(near, exp), device_id_type=MESH)
    own = pltpu.make_async_copy(d_ref.at[exp], buf.at[rep, exp], own_sem)
    own.start()
    load = pltpu.make_async_copy(w_ref, weights, w_sem)
    load.start()
    pl.semaphore_wait(barrier, n_exp + 1)

    far, near = n_rep // 2, n_rep - 1 - n_rep // 2
    hops = [[far if (k % 4 in (0, 3)) == (way == 0) else near for k in range(n_exp)] for way in (0, 1)]

    def origin(way, h):
        return ring_index((pos + n_rep - (h if way == 0 else n_rep - h)) % n_rep, n_rep)

    def ring(way, h, k):
        block = buf.at[origin(way, h), peer(k, -1)]
        return pltpu.make_async_remote_copy(
            src_ref=d_ref.at[exp] if h == 0 and k == 0 else block,
            dst_ref=block,
            send_sem=r_send.at[way, h, k],
            recv_sem=r_recv.at[way, h, k],
            device_id=(ahead if way == 0 else behind, exp),
            device_id_type=MESH,
        )

    def apply(source, k):
        at = (source, peer(k, -1))
        out_ref[at] = (weights[at].astype(jnp.float32) + buf[at].astype(jnp.float32)).astype(jnp.bfloat16)

    sent = []

    def forward(way, h, k):
        if h < hops[way][k]:
            copy = ring(way, h, k)
            copy.start()
            sent.append(copy)

    for way in (0, 1):
        forward(way, 0, 0)
    swaps = {}
    for k in list(range(CORES, n_exp)) + list(range(1, CORES)):
        swaps[k] = pltpu.make_async_remote_copy(
            src_ref=d_ref.at[peer(k, 1)],
            dst_ref=buf.at[rep, exp],
            send_sem=p_send.at[k],
            recv_sem=p_recv.at[k],
            device_id=(rep, peer(k, 1)),
            device_id_type=MESH,
        )
        swaps[k].start()

    for k in range(1, n_exp):
        swaps[k].wait_recv()
        for way in (0, 1):
            forward(way, 0, k)
    own.wait()
    load.wait()
    for k in range(n_exp):
        apply(rep, k)
    for h in range(1, far + 1):
        for k in range(n_exp):
            for way in (0, 1):
                if h <= hops[way][k]:
                    ring(way, h - 1, k).wait_recv()
                    forward(way, h, k)
                    apply(origin(way, h), k)
    for k in range(1, n_exp):
        swaps[k].wait_send()
    for copy in sent:
        copy.wait_send()


def exchange(n_rep, n_exp, delta, weights):
    slots, rows, columns = delta.shape
    whole = (n_rep, n_exp, rows, columns)
    size = n_rep * n_exp * rows * columns * 2
    far = n_rep // 2
    return pl.pallas_call(
        functools.partial(exchange_kernel, n_rep, n_exp),
        out_shape=jax.ShapeDtypeStruct(whole, jnp.bfloat16),
        in_specs=[pl.BlockSpec(memory_space=pltpu.HBM)] * 2,
        out_specs=pl.BlockSpec(memory_space=pltpu.VMEM),
        scratch_shapes=[
            pltpu.VMEM(whole, jnp.bfloat16),
            pltpu.VMEM(whole, jnp.bfloat16),
            pltpu.SemaphoreType.DMA(()),
            pltpu.SemaphoreType.DMA(()),
            pltpu.SemaphoreType.DMA((n_exp,)),
            pltpu.SemaphoreType.DMA((n_exp,)),
            pltpu.SemaphoreType.DMA((2, far, n_exp)),
            pltpu.SemaphoreType.DMA((2, far, n_exp)),
        ],
        compiler_params=pltpu.CompilerParams(
            collective_id=0, has_side_effects=True, vmem_limit_bytes=50 * 1024 * 1024
        ),
        cost_estimate=pl.CostEstimate(flops=0, bytes_accessed=3 * size, transcendentals=0),
        name="exchange",
    )(delta, weights.reshape(whole))


def exchange_by_collectives(delta):
    received = lax.all_to_all(delta, "expert", split_axis=0, concat_axis=0, tiled=True)
    return lax.all_gather(received, "replica", axis=0, tiled=False)


def shards(
    n_rep,
    n_exp,
    master,
    first_moment,
    second_moment,
    gradient,
    scale_exponent,
    slot_expert,
    expert_owner,
    serving_weights,
):
    master_out, first_out, second_out, delta = local_step(
        slot_expert[0, 0],
        expert_owner,
        master[0, 0],
        first_moment[0, 0],
        second_moment[0, 0],
        gradient[0, 0],
        scale_exponent[0, 0],
    )
    rows = master.shape[3]
    if rows % 16 == 0 and n_rep % 2 == 0 and n_exp % CORES == 0:
        serving_out = exchange(n_rep, n_exp, delta, serving_weights).reshape(serving_weights.shape)
    else:
        added = exchange_by_collectives(delta).reshape(serving_weights.shape).astype(jnp.float32)
        serving_out = (serving_weights.astype(jnp.float32) + added).astype(jnp.bfloat16)
    return (master_out[None, None], first_out[None, None], second_out[None, None], serving_out)


def solution(mesh):
    flat = P("replica", "expert", None, None, None)
    in_specs = (flat, flat, flat, flat, flat, P("replica", "expert", None), P(), P("expert", None, None))
    out_specs = (flat, flat, flat, P("expert", None, None))
    body = functools.partial(shards, mesh.shape["replica"], mesh.shape["expert"])
    return jax.shard_map(body, mesh=mesh, in_specs=in_specs, out_specs=out_specs, check_vma=False)
```

```python
import functools

import jax
import jax.numpy as jnp
from jax import lax
from jax.experimental import pallas as pl
from jax.experimental.pallas import tpu as pltpu
from jax.sharding import PartitionSpec as P

MESH = pl.DeviceIdType.MESH
CORES = 2


def adam(master, first_moment, second_moment, gradient):
    grad_full = gradient.astype(jnp.float32)
    first_out = 0.9 * first_moment + 0.1 * grad_full
    second_out = 0.95 * second_moment + 0.05 * grad_full * grad_full
    corr_first = 1.0 / (1.0 - 0.9**10)
    corr_second = 1.0 / (1.0 - 0.95**10)
    update = first_out * corr_first / (jnp.sqrt(second_out * corr_second) + 1e-08) + 0.1 * master
    delta = -0.1 * update
    return master + delta, first_out, second_out, delta


def adam_kernel(
    slot_ref, owner_ref, m_ref, f_ref, s_ref, g_ref, e_ref, mo_ref, fo_ref, so_ref, d_ref,
    m_in, f_in, s_in, g_in, e_in, m_new, f_new, s_new, e_sem, in_sem, out_sem,
):
    slots, _, columns = m_in.shape
    blocks = e_in.shape[0]
    width = columns // blocks
    exponents = pltpu.make_async_copy(e_ref, e_in, e_sem)
    exponents.start()
    pairs = ((m_ref, m_in), (f_ref, f_in), (s_ref, s_in), (g_ref, g_in))
    loads = [
        [pltpu.make_async_copy(src.at[s], dst.at[s], in_sem.at[i, s]) for i, (src, dst) in enumerate(pairs)]
        for s in range(slots)
    ]
    for copies in loads:
        for copy in copies:
            copy.start()
    exponents.wait()
    stores = []
    for s, copies in enumerate(loads):
        target = owner_ref[slot_ref[s]]
        limits = (jnp.left_shift(1, 7 - e_in[:, s, :]).astype(jnp.float32) * (8.0 / 128.0)).T
        for copy in copies:
            copy.wait()
        for b in range(blocks):
            cols = slice(b * width, (b + 1) * width)
            at = (s, slice(None), cols)
            m_new[at], f_new[at], s_new[at], delta = adam(m_in[at], f_in[at], s_in[at], g_in[at])
            limit = limits[:, b : b + 1]
            d_ref[target, :, cols] = jnp.minimum(jnp.maximum(delta, -limit), limit).astype(jnp.bfloat16)
        for i, (src, dst) in enumerate(((m_new, mo_ref), (f_new, fo_ref), (s_new, so_ref))):
            stores.append(pltpu.make_async_copy(src.at[s], dst.at[s], out_sem.at[i, s]))
            stores[-1].start()
    for copy in stores:
        copy.wait()


def local_step(slot_expert, expert_owner, master, first_moment, second_moment, gradient, scale_exponent):
    slots = master.shape[0]
    by_block = jnp.transpose(scale_exponent, (2, 0, 1))
    flat = jax.ShapeDtypeStruct(master.shape, jnp.float32)
    held = pltpu.VMEM(master.shape, jnp.float32)
    return pl.pallas_call(
        adam_kernel,
        in_specs=[pl.BlockSpec(memory_space=pltpu.SMEM)] * 2 + [pl.BlockSpec(memory_space=pl.ANY)] * 5,
        out_specs=[pl.BlockSpec(memory_space=pl.ANY)] * 3 + [pl.BlockSpec(memory_space=pltpu.VMEM)],
        out_shape=[flat, flat, flat, jax.ShapeDtypeStruct(master.shape, jnp.bfloat16)],
        scratch_shapes=[
            held,
            held,
            held,
            pltpu.VMEM(master.shape, jnp.bfloat16),
            pltpu.VMEM(by_block.shape, jnp.int32),
            held,
            held,
            held,
            pltpu.SemaphoreType.DMA(()),
            pltpu.SemaphoreType.DMA((4, slots)),
            pltpu.SemaphoreType.DMA((3, slots)),
        ],
        compiler_params=pltpu.CompilerParams(vmem_limit_bytes=118 * 512 * 1024),
        name="adam_step",
    )(slot_expert, expert_owner, master, first_moment, second_moment, gradient, by_block)


def ring_position(index, count):
    return (index // 2) * (1 - index % 2) + (count - 1 - index // 2) * (index % 2)


def ring_index(position, count):
    back = position // (count // 2)
    return 2 * position * (1 - back) + (2 * (count - 1 - position) + 1) * back


def exchange_kernel(
    n_rep, n_exp, d_ref, w_ref, out_ref, buf, weights, own_sem, w_sem, p_send, p_recv, r_send, r_recv
):
    rep = lax.axis_index("replica")
    exp = lax.axis_index("expert")
    pos = ring_position(rep, n_rep)
    ahead = ring_index((pos + 1) % n_rep, n_rep)
    behind = ring_index((pos + n_rep - 1) % n_rep, n_rep)
    chips = n_exp // CORES
    chip, core = exp // CORES, exp % CORES

    def peer(k, sign):
        dc, dk = k // CORES, k % CORES
        return ((chip + sign * dc + chips) % chips) * CORES + (core + sign * dk + CORES) % CORES

    barrier = pltpu.get_barrier_semaphore()
    for k in range(1, n_exp):
        pl.semaphore_signal(barrier, inc=1, device_id=(rep, peer(k, 1)), device_id_type=MESH)
    for near in (ahead, behind):
        pl.semaphore_signal(barrier, inc=1, device_id=(near, exp), device_id_type=MESH)
    own = pltpu.make_async_copy(d_ref.at[exp], buf.at[rep, exp], own_sem)
    own.start()
    load = pltpu.make_async_copy(w_ref, weights, w_sem)
    load.start()
    pl.semaphore_wait(barrier, n_exp + 1)

    far, near = n_rep // 2, n_rep - 1 - n_rep // 2
    hops = [[far if (k % 4 in (0, 3)) == (way == 0) else near for k in range(n_exp)] for way in (0, 1)]

    def origin(way, h):
        return ring_index((pos + n_rep - (h if way == 0 else n_rep - h)) % n_rep, n_rep)

    def ring(way, h, k):
        block = buf.at[origin(way, h), peer(k, -1)]
        return pltpu.make_async_remote_copy(
            src_ref=d_ref.at[exp] if h == 0 and k == 0 else block,
            dst_ref=block,
            send_sem=r_send.at[way, h, k],
            recv_sem=r_recv.at[way, h, k],
            device_id=(ahead if way == 0 else behind, exp),
            device_id_type=MESH,
        )

    def apply(source, k):
        at = (source, peer(k, -1))
        out_ref[at] = (weights[at].astype(jnp.float32) + buf[at].astype(jnp.float32)).astype(jnp.bfloat16)

    sent = []

    def forward(way, h, k):
        if h < hops[way][k]:
            copy = ring(way, h, k)
            copy.start()
            sent.append(copy)

    for way in (0, 1):
        forward(way, 0, 0)
    swaps = {}
    for k in list(range(CORES, n_exp)) + list(range(1, CORES)):
        swaps[k] = pltpu.make_async_remote_copy(
            src_ref=d_ref.at[peer(k, 1)],
            dst_ref=buf.at[rep, exp],
            send_sem=p_send.at[k],
            recv_sem=p_recv.at[k],
            device_id=(rep, peer(k, 1)),
            device_id_type=MESH,
        )
        swaps[k].start()

    for k in range(1, n_exp):
        swaps[k].wait_recv()
        for way in (0, 1):
            forward(way, 0, k)
    own.wait()
    load.wait()
    for k in range(n_exp):
        apply(rep, k)
    for h in range(1, far + 1):
        for k in range(n_exp):
            for way in (0, 1):
                if h <= hops[way][k]:
                    ring(way, h - 1, k).wait_recv()
                    forward(way, h, k)
                    apply(origin(way, h), k)
    for k in range(1, n_exp):
        swaps[k].wait_send()
    for copy in sent:
        copy.wait_send()


def exchange(n_rep, n_exp, delta, weights):
    slots, rows, columns = delta.shape
    whole = (n_rep, n_exp, rows, columns)
    size = n_rep * n_exp * rows * columns * 2
    far = n_rep // 2
    return pl.pallas_call(
        functools.partial(exchange_kernel, n_rep, n_exp),
        out_shape=jax.ShapeDtypeStruct(whole, jnp.bfloat16),
        in_specs=[pl.BlockSpec(memory_space=pltpu.HBM)] * 2,
        out_specs=pl.BlockSpec(memory_space=pltpu.VMEM),
        scratch_shapes=[
            pltpu.VMEM(whole, jnp.bfloat16),
            pltpu.VMEM(whole, jnp.bfloat16),
            pltpu.SemaphoreType.DMA(()),
            pltpu.SemaphoreType.DMA(()),
            pltpu.SemaphoreType.DMA((n_exp,)),
            pltpu.SemaphoreType.DMA((n_exp,)),
            pltpu.SemaphoreType.DMA((2, far, n_exp)),
            pltpu.SemaphoreType.DMA((2, far, n_exp)),
        ],
        compiler_params=pltpu.CompilerParams(
            collective_id=0, has_side_effects=True, vmem_limit_bytes=50 * 1024 * 1024
        ),
        cost_estimate=pl.CostEstimate(flops=0, bytes_accessed=3 * size, transcendentals=0),
        name="exchange",
    )(delta, weights.reshape(whole))


def exchange_by_collectives(delta):
    received = lax.all_to_all(delta, "expert", split_axis=0, concat_axis=0, tiled=True)
    return lax.all_gather(received, "replica", axis=0, tiled=False)


def shards(
    n_rep,
    n_exp,
    master,
    first_moment,
    second_moment,
    gradient,
    scale_exponent,
    slot_expert,
    expert_owner,
    serving_weights,
):
    master_out, first_out, second_out, delta = local_step(
        slot_expert[0, 0],
        expert_owner,
        master[0, 0],
        first_moment[0, 0],
        second_moment[0, 0],
        gradient[0, 0],
        scale_exponent[0, 0],
    )
    rows = master.shape[3]
    if rows % 16 == 0 and n_rep % 2 == 0 and n_exp % CORES == 0:
        serving_out = exchange(n_rep, n_exp, delta, serving_weights).reshape(serving_weights.shape)
    else:
        added = exchange_by_collectives(delta).reshape(serving_weights.shape).astype(jnp.float32)
        serving_out = (serving_weights.astype(jnp.float32) + added).astype(jnp.bfloat16)
    return (master_out[None, None], first_out[None, None], second_out[None, None], serving_out)


def solution(mesh):
    flat = P("replica", "expert", None, None, None)
    in_specs = (flat, flat, flat, flat, flat, P("replica", "expert", None), P(), P("expert", None, None))
    out_specs = (flat, flat, flat, P("expert", None, None))
    body = functools.partial(shards, mesh.shape["replica"], mesh.shape["expert"])
    return jax.shard_map(body, mesh=mesh, in_specs=in_specs, out_specs=out_specs, check_vma=False)
```
